32 devices in a mesh: orb: 8 (over z, core), aux: 4 (over y, x).
Axes of the slice: x: 2, y: 2, z: 4, core: 2. Of those that a mesh axis runs over, the one named last changes fastest.
Arguments:
- three_centre: bfloat16 [32, 4096, 384], P('aux', 'orb'), may hold values from -6 to 6
- b_screen: int32 [32, 3], P('orb'), may hold values 0 or 1
- g_occ: bfloat16 [4096, 384], P('orb'), may hold values from -0.0068359375 to 0.0068359375
- occ_screen: int32 [32, 3], P('orb'), may hold values 0 or 1
- g_vir: bfloat16 [4096, 384], P('orb'), may hold values from -0.0068359375 to 0.0068359375
- vir_screen: int32 [32, 3], P('orb'), may hold values 0 or 1
Outputs:
- response: float32 [32, 32], P('aux')
The draws below stay inside these ranges and needn't reach their ends.
All inputs are finite; a program needn't handle non-finite values. No bound on the sum of `b_screen` or of `occ_screen` or of `vir_screen` on one device may be relied on, other than what follows from the above.
Results may differ from the reference program's by a relative error of at most 0.0029.
Values may be sent and summed in bfloat16 or wider, within the bound.
A program may use at most 128 MiB of HBM per device.

```python
import jax
import jax.numpy as jnp
from jax import lax

BLK = 128
ORB = 4096
NOB = 32
AUXB = 32


def touch_ends(entries, key, least, top_value):
    index_at = [jax.random.randint(jax.random.fold_in(key, axis), (), 0, length) for axis, length in enumerate(entries.shape)]
    longest = entries.shape.index(max(entries.shape))
    next_to = index_at[:longest] + [(index_at[longest] + 1) % entries.shape[longest]] + index_at[longest + 1:]
    return entries.at[tuple(index_at)].set(least).at[tuple(next_to)].set(top_value)


def level_of(key, dims, cuts, smallest, largest):
    gain = 1.0
    for position, parts in cuts:
        steps = jax.random.uniform(jax.random.fold_in(jax.random.fold_in(key, 6), position), (parts,), jnp.float32, smallest / len(cuts), largest / len(cuts))
        gain = gain * jnp.repeat(jnp.exp(steps), dims[position] // parts).reshape((-1,) + (1,) * (len(dims) - 1 - position))
    return gain


def gaussian(stream_key, dims, scale, bound, cuts=(), kind=jnp.bfloat16):
    result = scale * jax.random.normal(stream_key, dims, jnp.float32)
    if cuts:
        result = result * level_of(stream_key, dims, cuts, -0.22, 0.18)
    return jnp.clip(result, -bound, bound).astype(kind)


def setup_inputs(seed: int = 0) -> dict:
    arg_keys = jax.random.split(jax.random.key(seed), 7)
    three_centre = gaussian(arg_keys[0], (AUXB, ORB, 3 * BLK), 1.0, 6.0, ((0, 4), (1, 8)))
    b_screen = touch_ends((jax.random.randint(arg_keys[1], (NOB, 3), 0, 4) < 3).astype(jnp.int32), jax.random.fold_in(arg_keys[1], 1), 0, 1)
    g_occ = gaussian(arg_keys[2], (ORB, 3 * BLK), (3 * BLK * 2048) ** -0.5, 0.0068359375, ((0, 8),))
    occ_screen = touch_ends((jax.random.randint(arg_keys[3], (NOB, 3), 0, 4) < 3).astype(jnp.int32), jax.random.fold_in(arg_keys[3], 1), 0, 1)
    g_vir = gaussian(arg_keys[4], (ORB, 3 * BLK), (3 * BLK * 2048) ** -0.5, 0.0068359375, ((0, 8),))
    vir_screen = touch_ends((jax.random.randint(arg_keys[5], (NOB, 3), 0, 4) < 3).astype(jnp.int32), jax.random.fold_in(arg_keys[5], 1), 0, 1)
    return {"three_centre": three_centre, "b_screen": b_screen, "g_occ": g_occ, "occ_screen": occ_screen, "g_vir": g_vir, "vir_screen": vir_screen}


def kept_tiles(values, screen, nob):
    blocks = jnp.arange(nob, dtype=jnp.int32)[:, None] + jnp.arange(3, dtype=jnp.int32)[None, :] - 1
    live = (screen == 1) & (blocks >= 0) & (blocks < nob)
    mask = jnp.repeat(jnp.repeat(live, BLK, axis=0), BLK, axis=1)
    return jnp.where(mask, values, jnp.zeros((), values.dtype))


def reference(three_centre, b_screen, g_occ, occ_screen, g_vir, vir_screen):
    nob = g_occ.shape[0] // BLK
    naux = three_centre.shape[0]
    width = 3 * BLK
    b_mask = kept_tiles(jnp.ones(g_occ.shape, jnp.float32), b_screen, nob)
    kept_b = jnp.where(b_mask[None] > 0.5, three_centre, jnp.zeros((), three_centre.dtype))
    kept_o = kept_tiles(g_occ, occ_screen, nob)
    kept_v = kept_tiles(g_vir, vir_screen, nob)
    b_pad = jnp.pad(kept_b, ((0, 0), (BLK, BLK), (0, 0)))
    v_pad = jnp.pad(kept_v, ((BLK, BLK), (0, 0)))
    zero = jnp.int32(0)

    def one_block(total, block):
        start = (block * BLK).astype(jnp.int32)
        rows_b = lax.dynamic_slice(kept_b, (zero, start, zero), (naux, BLK, width)).astype(jnp.float32)
        occ_rows = lax.dynamic_slice(kept_o, (start, zero), (BLK, width)).astype(jnp.float32)
        left = jnp.zeros((naux, BLK, 5 * BLK), jnp.float32)
        right = jnp.zeros((naux, BLK, 5 * BLK), jnp.float32)
        for slot in range(3):
            shifted = ((block + slot) * BLK).astype(jnp.int32)
            vir_rows = lax.dynamic_slice(v_pad, (shifted, zero), (BLK, width)).astype(jnp.float32)
            term = jnp.einsum("pil,lk->pik", rows_b[:, :, slot * BLK:(slot + 1) * BLK], vir_rows)
            left = left.at[:, :, slot * BLK:slot * BLK + width].add(term)
            near_b = lax.dynamic_slice(b_pad, (zero, shifted, zero), (naux, BLK, width)).astype(jnp.float32)
            term = jnp.einsum("in,qnk->qik", occ_rows[:, slot * BLK:(slot + 1) * BLK], near_b)
            right = right.at[:, :, slot * BLK:slot * BLK + width].add(term)
        right_b = right.astype(jnp.bfloat16).astype(jnp.float32).reshape(naux, BLK * 5 * BLK)
        left_f = left.reshape(naux, BLK * 5 * BLK)
        total = total + lax.dot_general(left_f, right_b, (((1,), (1,)), ((), ())),
                                        precision=lax.Precision.HIGHEST, preferred_element_type=jnp.float32)
        return total, None

    total, unused = lax.scan(one_block, jnp.zeros((naux, naux), jnp.float32), jnp.arange(nob, dtype=jnp.int32))
    return total
```

```python
import jax
import jax.numpy as jnp
from jax import lax
from jax.sharding import PartitionSpec as P


def with_halo(block, sides, width):
    for axis, dim in sides:
        count = lax.axis_size(axis)
        forward = [(i, i + 1) for i in range(count - 1)]
        backward = [(target, source) for source, target in forward]
        low = lax.ppermute(
            lax.slice_in_dim(block, block.shape[dim] - width, None, axis=dim), axis, forward
        )
        high = lax.ppermute(lax.slice_in_dim(block, 0, width, axis=dim), axis, backward)
        block = jnp.concatenate([low, block, high], axis=dim)
    return block


def tile_mask(screen, first, nob, block_size):
    count = screen.shape[0]
    blocks = (
        first
        + jnp.arange(count, dtype=jnp.int32)[:, None]
        + jnp.arange(3, dtype=jnp.int32)[None, :]
        - 1
    )
    live = (screen == 1) & (blocks >= 0) & (blocks < nob)
    return jnp.repeat(jnp.repeat(live, block_size, axis=0), block_size, axis=1)


def per_device(three_centre, b_screen, g_occ, occ_screen, g_vir, vir_screen):
    aux_dev, rows, width = three_centre.shape
    block_size = width // 3
    nbd = rows // block_size
    nob = nbd * lax.axis_size("orb")
    first = lax.axis_index("orb") * nbd
    nothing = jnp.zeros((), jnp.bfloat16)
    every_b = lax.all_to_all(three_centre, "aux", split_axis=1, concat_axis=0, tiled=True)
    b_mask = tile_mask(b_screen, first, nob, block_size)[None]
    kept_b = jnp.where(b_mask, three_centre, nothing)
    kept_o = jnp.where(tile_mask(occ_screen, first, nob, block_size), g_occ, nothing)
    kept_v = jnp.where(tile_mask(vir_screen, first, nob, block_size), g_vir, nothing)
    wide_b = with_halo(kept_b, (("orb", 1),), block_size)
    wide_v = with_halo(kept_v, (("orb", 0),), block_size)
    right = jnp.zeros((aux_dev, nbd, block_size, 5 * block_size), jnp.float32)
    for slot in range(3):
        lower = slot * block_size
        occ_slot = kept_o[:, lower : lower + block_size].reshape(nbd, block_size, block_size)
        near_b = wide_b[:, lower : lower + rows].reshape(aux_dev, nbd, block_size, width)
        term = jnp.einsum("jin,qjnk->qjik", occ_slot, near_b, preferred_element_type=jnp.float32)
        right = right.at[..., lower : lower + width].add(term)
    right_b = right.astype(jnp.bfloat16)
    parts = []
    for slot in range(3):
        lower = slot * block_size
        vir_rows = wide_v[lower : lower + rows].reshape(nbd, block_size, width)
        parts.append(
            jnp.einsum(
                "qjik,jlk->qjil",
                right_b[..., lower : lower + width],
                vir_rows,
                preferred_element_type=jnp.float32,
            )
        )
    w = jnp.concatenate(parts, axis=-1).reshape(aux_dev, rows, width)
    w = jnp.where(b_mask, w, 0.0).astype(jnp.bfloat16)
    every_w = lax.all_to_all(w, "aux", split_axis=1, concat_axis=0, tiled=True)
    partial_value = lax.dot_general(
        every_b,
        every_w,
        (((1, 2), (1, 2)), ((), ())),
        preferred_element_type=jnp.float32,
    )
    summed = lax.psum(partial_value, ("orb", "aux"))
    return lax.dynamic_slice_in_dim(summed, lax.axis_index("aux") * aux_dev, aux_dev, 0)


def solution(mesh):
    in_specs = (
        P("aux", "orb", None),
        P("orb", None),
        P("orb", None),
        P("orb", None),
        P("orb", None),
        P("orb", None),
    )
    out_specs = P("aux", None)
    return jax.shard_map(
        per_device, mesh=mesh, in_specs=in_specs, out_specs=out_specs, check_vma=False
    )
```

```python
import functools

import jax
import jax.numpy as jnp
from jax import lax
from jax.experimental import pallas as pl
from jax.experimental.pallas import tpu as pltpu
from jax.sharding import PartitionSpec as P

MESH = pl.DeviceIdType.MESH
TILE = 16
ORDER_LANES = 128


def xor(value, step, count):
    result = 0
    bit = 1
    while bit < count:
        result = result + lax.rem(value // bit + step // bit, 2) * bit
        bit *= 2
    return result


def kernel(
    n_orb,
    n_aux,
    b_hbm,
    o_ref,
    v_ref,
    bs_ref,
    os_ref,
    vs_ref,
    out_ref,
    kb,
    lo_b,
    hi_b,
    ko,
    kv,
    lo_v,
    hi_v,
    right,
    every_b,
    own_w,
    every_w,
    part,
    part_aux,
    part_orb,
    load_sem,
    own_sem,
    b_send,
    b_recv,
    halo_send,
    halo_recv,
    w_send,
    w_recv,
    p_send,
    p_recv,
    q_send,
    q_recv,
):
    aux_dev, rows, width = b_hbm.shape
    blk = width // 3
    nbd = rows // blk
    share = rows // n_aux
    per_block = blk // share
    naux = n_aux * aux_dev
    lanes = part.shape[-1]
    orb = lax.axis_index("orb")
    aux = lax.axis_index("aux")

    edges = [0, nbd - 1] if nbd > 1 else [0]
    inner = [j for j in range(nbd) if j not in edges]
    loads = {}
    for j in edges + inner:
        loads[j] = pltpu.make_async_copy(
            b_hbm.at[:, j * blk : (j + 1) * blk, :],
            kb.at[:, j * blk : (j + 1) * blk, :],
            load_sem.at[j],
        )
        loads[j].start()

    barrier = pltpu.get_barrier_semaphore()
    for k in range(1, n_aux):
        pl.semaphore_signal(
            barrier, inc=1, device_id=(orb, xor(aux, k, n_aux)), device_id_type=MESH
        )
    for k in range(1, n_orb):
        pl.semaphore_signal(
            barrier, inc=1, device_id=(lax.rem(orb + k, n_orb), aux), device_id_type=MESH
        )
    pl.semaphore_wait(barrier, n_aux + n_orb - 2)

    b_copies = []
    for k in range(n_aux - 1, 0, -1):
        peer = xor(aux, k, n_aux)
        copy = pltpu.make_async_remote_copy(
            src_ref=b_hbm.at[:, pl.ds(pl.multiple_of(peer * share, share), share), :],
            dst_ref=every_b.at[aux],
            send_sem=b_send.at[k],
            recv_sem=b_recv.at[k],
            device_id=(orb, peer),
            device_id_type=MESH,
        )
        copy.start()
        b_copies.append(copy)
    own_copy = pltpu.make_async_copy(
        b_hbm.at[:, pl.ds(pl.multiple_of(aux * share, share), share), :],
        every_b.at[aux],
        own_sem,
    )
    own_copy.start()

    has_low = jnp.where(orb > 0, 1, 0)
    has_high = jnp.where(orb < n_orb - 1, 1, 0)

    def factor(screen, j, t):
        value = screen[j, t]
        if j == 0 and t == 0:
            value = value * has_low
        if j == nbd - 1 and t == 2:
            value = value * has_high
        return value.astype(jnp.float32)

    def scaled(tile, scale):
        return (tile.astype(jnp.float32) * scale).astype(jnp.bfloat16)

    for j in range(nbd):
        for t in range(3):
            at = (slice(j * blk, (j + 1) * blk), slice(t * blk, (t + 1) * blk))
            kv[at] = scaled(v_ref[at], factor(vs_ref, j, t))
            ko[at] = scaled(o_ref[at], factor(os_ref, j, t))

    def screen_block(j):
        loads[j].wait()
        scales = [factor(bs_ref, j, t) for t in range(3)]

        def body(q, carry):
            for t in range(3):
                at = (q, slice(j * blk, (j + 1) * blk), slice(t * blk, (t + 1) * blk))
                kb[at] = scaled(kb[at], scales[t])
            return carry

        lax.fori_loop(0, aux_dev, body, 0)

    for j in edges:
        screen_block(j)

    def halo(index, source, target, peer):
        return pltpu.make_async_remote_copy(
            src_ref=source,
            dst_ref=target,
            send_sem=halo_send.at[index],
            recv_sem=halo_recv.at[index],
            device_id=(peer, aux),
            device_id_type=MESH,
        )

    below = lax.rem(orb + n_orb - 1, n_orb)
    above = lax.rem(orb + 1, n_orb)
    last = slice(rows - blk, rows)
    up = [
        halo(0, kv.at[last], lo_v, above),
        halo(1, kb.at[:, last, :], lo_b, above),
    ]
    down = [
        halo(2, kv.at[0:blk], hi_v, below),
        halo(3, kb.at[:, 0:blk, :], hi_b, below),
    ]

    @pl.when(orb < n_orb - 1)
    def _():
        for copy in up:
            copy.start()

    @pl.when(orb > 0)
    def _():
        for copy in down:
            copy.start()

    @pl.when(orb == 0)
    def _():
        lo_v[...] = jnp.zeros_like(lo_v)
        lo_b[...] = jnp.zeros_like(lo_b)

    @pl.when(orb == n_orb - 1)
    def _():
        hi_v[...] = jnp.zeros_like(hi_v)
        hi_b[...] = jnp.zeros_like(hi_b)

    for j in inner:
        screen_block(j)

    def near_b(j, q):
        if j < 0:
            return lo_b[q]
        if j >= nbd:
            return hi_b[q]
        return kb[q, j * blk : (j + 1) * blk, :]

    def near_v(j):
        if j < 0:
            return lo_v[...]
        if j >= nbd:
            return hi_v[...]
        return kv[j * blk : (j + 1) * blk, :]

    def w_copy(p):
        return pltpu.make_async_remote_copy(
            src_ref=own_w.at[p],
            dst_ref=every_w.at[aux],
            send_sem=w_send.at[p],
            recv_sem=w_recv.at[aux],
            device_id=(orb, p),
            device_id_type=MESH,
        )

    def one_block(j):
        def body(q, carry):
            terms = []
            for s in range(3):
                occ = ko[j * blk : (j + 1) * blk, s * blk : (s + 1) * blk]
                terms.append(
                    jnp.dot(occ, near_b(j + s - 1, q), preferred_element_type=jnp.float32)
                )
            for u in range(5):
                total = None
                for s in range(3):
                    t = u - s
                    if 0 <= t < 3:
                        piece = terms[s][:, t * blk : (t + 1) * blk]
                        total = piece if total is None else total + piece
                right[q, :, u * blk : (u + 1) * blk] = total.astype(jnp.bfloat16)
            return carry

        lax.fori_loop(0, aux_dev, body, 0)
        for s in range(3):
            rows_r = right[:, :, s * blk : s * blk + width].reshape(aux_dev * blk, width)
            value = lax.dot_general(
                rows_r,
                near_v(j + s - 1),
                (((1,), (1,)), ((), ())),
                preferred_element_type=jnp.float32,
            )
            value = (value * factor(bs_ref, j, s)).astype(jnp.bfloat16)
            value = value.reshape(aux_dev, blk, blk)
            for k in range(per_block):
                own_w[j * per_block + k, :, :, s * blk : (s + 1) * blk] = value[
                    :, k * share : (k + 1) * share
                ]
        for k in range(per_block):
            p = j * per_block + k

            @pl.when(aux != p)
            def _():
                w_copy(p).start()

    for j in inner:
        one_block(j)

    @pl.when(orb > 0)
    def _():
        for copy in up:
            copy.wait_recv()

    @pl.when(orb < n_orb - 1)
    def _():
        for copy in down:
            copy.wait_recv()

    for j in edges:
        one_block(j)

    own_copy.wait()
    for copy in b_copies:
        copy.wait_recv()

    pair_rows = lax.broadcasted_iota(jnp.int32, (naux * TILE, aux_dev * TILE), 0)
    pair_cols = lax.broadcasted_iota(jnp.int32, (naux * TILE, aux_dev * TILE), 1)
    same = (pair_rows & (TILE - 1)) == (pair_cols & (TILE - 1))
    pick_rows = lax.broadcasted_iota(jnp.int32, (aux_dev * TILE, lanes), 0) // TILE
    pick_cols = lax.broadcasted_iota(jnp.int32, (aux_dev * TILE, lanes), 1)

    def pairs(ref, source):
        total = None
        for t in range(share // TILE):
            cut = slice(t * TILE, (t + 1) * TILE)
            left = every_b[:, :, cut, :].reshape(naux * TILE, width)
            other = ref[source, :, cut, :].reshape(aux_dev * TILE, width)
            term = lax.dot_general(
                left, other, (((1,), (1,)), ((), ())), preferred_element_type=jnp.float32
            )
            total = term if total is None else total + term
        total = jnp.where(same, total, 0.0).reshape(naux, TILE, aux_dev * TILE)
        total = jnp.sum(total, axis=1)
        pick = jnp.where(pick_rows + source * aux_dev == pick_cols, 1.0, 0.0)
        value = jnp.dot(
            total, pick, precision=lax.Precision.HIGHEST, preferred_element_type=jnp.float32
        )
        return value.reshape(n_aux, aux_dev, lanes)

    part[...] = pairs(own_w, aux)
    for k in range(1, n_aux):
        source = xor(aux, k, n_aux)
        pltpu.make_async_remote_copy(
            src_ref=own_w.at[source],
            dst_ref=every_w.at[source],
            send_sem=w_send.at[source],
            recv_sem=w_recv.at[source],
            device_id=(orb, source),
            device_id_type=MESH,
        ).wait_recv()
        part[...] += pairs(every_w, source)

    p_copies = []
    for k in range(1, n_aux):
        peer = xor(aux, k, n_aux)
        copy = pltpu.make_async_remote_copy(
            src_ref=part.at[peer],
            dst_ref=part_aux.at[k],
            send_sem=p_send.at[k],
            recv_sem=p_recv.at[k],
            device_id=(orb, peer),
            device_id_type=MESH,
        )
        copy.start()
        p_copies.append(copy)
    mine = part[aux]
    for k in range(1, n_aux):
        p_copies[k - 1].wait_recv()
        mine = mine + part_aux[k]
    part_orb[orb] = mine
    q_copies = []
    for k in range(1, n_orb):
        peer = lax.rem(orb + k, n_orb)
        copy = pltpu.make_async_remote_copy(
            src_ref=part_orb.at[orb],
            dst_ref=part_orb.at[orb],
            send_sem=q_send.at[k],
            recv_sem=q_recv.at[k],
            device_id=(peer, aux),
            device_id_type=MESH,
        )
        copy.start()
        q_copies.append(copy)
    for k in range(1, n_orb):
        source = lax.rem(orb + n_orb - k, n_orb)
        pltpu.make_async_remote_copy(
            src_ref=part_orb.at[source],
            dst_ref=part_orb.at[source],
            send_sem=q_send.at[k],
            recv_sem=q_recv.at[k],
            device_id=(source, aux),
            device_id_type=MESH,
        ).wait_recv()
    result = part_orb[0]
    for k in range(1, n_orb):
        result = result + part_orb[k]
    out_ref[...] = result[:, :naux]

    for copy in b_copies + p_copies + q_copies:
        copy.wait_send()

    @pl.when(orb < n_orb - 1)
    def _():
        for copy in up:
            copy.wait_send()

    @pl.when(orb > 0)
    def _():
        for copy in down:
            copy.wait_send()

    for p in range(n_aux):

        @pl.when(aux != p)
        def _():
            w_copy(p).wait_send()


def per_device(n_orb, n_aux, three_centre, b_screen, g_occ, occ_screen, g_vir, vir_screen):
    aux_dev, rows, width = three_centre.shape
    blk = width // 3
    share = rows // n_aux
    naux = n_aux * aux_dev
    lanes = -(-naux // ORDER_LANES) * ORDER_LANES
    bf16, f32 = jnp.bfloat16, jnp.float32
    vmem = pl.BlockSpec(memory_space=pltpu.VMEM)
    smem = pl.BlockSpec(memory_space=pltpu.SMEM)
    dma = pltpu.SemaphoreType.DMA
    flops = 4 * aux_dev * rows * width * width
    return pl.pallas_call(
        functools.partial(kernel, n_orb, n_aux),
        out_shape=jax.ShapeDtypeStruct((aux_dev, naux), f32),
        in_specs=[pl.BlockSpec(memory_space=pl.ANY), vmem, vmem, smem, smem, smem],
        out_specs=vmem,
        scratch_shapes=[
            pltpu.VMEM((aux_dev, rows, width), bf16),
            pltpu.VMEM((aux_dev, blk, width), bf16),
            pltpu.VMEM((aux_dev, blk, width), bf16),
            pltpu.VMEM((rows, width), bf16),
            pltpu.VMEM((rows, width), bf16),
            pltpu.VMEM((blk, width), bf16),
            pltpu.VMEM((blk, width), bf16),
            pltpu.VMEM((aux_dev, blk, 5 * blk), bf16),
            pltpu.VMEM((n_aux, aux_dev, share, width), bf16),
            pltpu.VMEM((n_aux, aux_dev, share, width), bf16),
            pltpu.VMEM((n_aux, aux_dev, share, width), bf16),
            pltpu.VMEM((n_aux, aux_dev, lanes), f32),
            pltpu.VMEM((n_aux, aux_dev, lanes), f32),
            pltpu.VMEM((n_orb, aux_dev, lanes), f32),
            dma((rows // blk,)),
            dma,
            dma((n_aux,)),
            dma((n_aux,)),
            dma((4,)),
            dma((4,)),
            dma((n_aux,)),
            dma((n_aux,)),
            dma((n_aux,)),
            dma((n_aux,)),
            dma((n_orb,)),
            dma((n_orb,)),
        ],
        compiler_params=pltpu.CompilerParams(
            collective_id=0, has_side_effects=True, vmem_limit_bytes=56 * 1024 * 1024
        ),
        cost_estimate=pl.CostEstimate(
            flops=flops, bytes_accessed=4 * aux_dev * rows * width, transcendentals=0
        ),
    )(three_centre, g_occ, g_vir, b_screen, occ_screen, vir_screen)


def solution(mesh):
    in_specs = (
        P("aux", "orb", None),
        P("orb", None),
        P("orb", None),
        P("orb", None),
        P("orb", None),
        P("orb", None),
    )
    out_specs = P("aux", None)
    body = functools.partial(per_device, mesh.shape["orb"], mesh.shape["aux"])
    return jax.shard_map(body, mesh=mesh, in_specs=in_specs, out_specs=out_specs, check_vma=False)
```

```python
import functools

import jax
import jax.numpy as jnp
from jax import lax
from jax.experimental import pallas as pl
from jax.experimental.pallas import tpu as pltpu
from jax.sharding import PartitionSpec as P

MESH = pl.DeviceIdType.MESH
TILE = 16
ORDER_LANES = 128


def xor(value, step, count):
    result = 0
    bit = 1
    while bit < count:
        result = result + lax.rem(value // bit + step // bit, 2) * bit
        bit *= 2
    return result


def kernel(
    n_orb,
    n_aux,
    b_hbm,
    o_hbm,
    v_hbm,
    bs_ref,
    os_ref,
    vs_ref,
    out_ref,
    kb,
    lo_b,
    hi_b,
    o_ref,
    v_ref,
    ko,
    kv,
    lo_v,
    hi_v,
    right,
    every_b,
    own_w,
    every_w,
    part,
    part_aux,
    part_orb,
    load_sem,
    own_sem,
    b_send,
    b_recv,
    halo_send,
    halo_recv,
    w_send,
    w_recv,
    p_send,
    p_recv,
    q_send,
    q_recv,
    g_sem,
    pair_acc,
):
    aux_dev, rows, width = b_hbm.shape
    blk = width // 3
    nbd = rows // blk
    share = rows // n_aux
    per_block = blk // share
    naux = n_aux * aux_dev
    lanes = part.shape[-1]
    orb = lax.axis_index("orb")
    aux = lax.axis_index("aux")

    pieces = min(4, share // TILE)
    piece = share // pieces
    edges = [0, nbd - 1] if nbd > 1 else [0]
    inner = [j for j in range(nbd) if j not in edges]
    loads = {}
    for j in edges + inner:
        loads[j] = pltpu.make_async_copy(
            b_hbm.at[:, j * blk : (j + 1) * blk, :],
            kb.at[:, j * blk : (j + 1) * blk, :],
            load_sem.at[j],
        )
        loads[j].start()

    v_load = pltpu.make_async_copy(v_hbm, v_ref, g_sem.at[0])
    o_load = pltpu.make_async_copy(o_hbm, o_ref, g_sem.at[1])
    v_load.start()
    o_load.start()

    barrier = pltpu.get_barrier_semaphore()
    for k in range(1, n_aux):
        pl.semaphore_signal(
            barrier, inc=1, device_id=(orb, xor(aux, k, n_aux)), device_id_type=MESH
        )
    for k in range(1, n_orb):
        pl.semaphore_signal(
            barrier, inc=1, device_id=(lax.rem(orb + k, n_orb), aux), device_id_type=MESH
        )
    pl.semaphore_wait(barrier, n_aux + n_orb - 2)

    b_copies = []
    for k in range(n_aux - 1, 0, -1):
        peer = xor(aux, k, n_aux)
        copy = pltpu.make_async_remote_copy(
            src_ref=b_hbm.at[:, pl.ds(pl.multiple_of(peer * share, share), share), :],
            dst_ref=every_b.at[aux],
            send_sem=b_send.at[k],
            recv_sem=b_recv.at[k],
            device_id=(orb, peer),
            device_id_type=MESH,
        )
        copy.start()
        b_copies.append(copy)
    own_copy = pltpu.make_async_copy(
        b_hbm.at[:, pl.ds(pl.multiple_of(aux * share, share), share), :],
        every_b.at[aux],
        own_sem,
    )
    own_copy.start()

    has_low = jnp.where(orb > 0, 1, 0)
    has_high = jnp.where(orb < n_orb - 1, 1, 0)

    def factor(screen, j, t):
        value = screen[j, t]
        if j == 0 and t == 0:
            value = value * has_low
        if j == nbd - 1 and t == 2:
            value = value * has_high
        return value.astype(jnp.float32)

    def scaled(tile, scale):
        return (tile.astype(jnp.float32) * scale).astype(jnp.bfloat16)

    v_load.wait()
    o_load.wait()
    for j in range(nbd):
        for t in range(3):
            at = (slice(j * blk, (j + 1) * blk), slice(t * blk, (t + 1) * blk))
            kv[at] = scaled(v_ref[at], factor(vs_ref, j, t))
            ko[at] = scaled(o_ref[at], factor(os_ref, j, t))

    def screen_block(j):
        loads[j].wait()
        scales = [factor(bs_ref, j, t) for t in range(3)]

        def body(q, carry):
            for t in range(3):
                at = (q, slice(j * blk, (j + 1) * blk), slice(t * blk, (t + 1) * blk))
                kb[at] = scaled(kb[at], scales[t])
            return carry

        lax.fori_loop(0, aux_dev, body, 0)

    for j in edges:
        screen_block(j)

    def halo(index, source, target, peer):
        return pltpu.make_async_remote_copy(
            src_ref=source,
            dst_ref=target,
            send_sem=halo_send.at[index],
            recv_sem=halo_recv.at[index],
            device_id=(peer, aux),
            device_id_type=MESH,
        )

    below = lax.rem(orb + n_orb - 1, n_orb)
    above = lax.rem(orb + 1, n_orb)
    last = slice(rows - blk, rows)
    up = [
        halo(0, kv.at[last], lo_v, above),
        halo(1, kb.at[:, last, :], lo_b, above),
    ]
    down = [
        halo(2, kv.at[0:blk], hi_v, below),
        halo(3, kb.at[:, 0:blk, :], hi_b, below),
    ]

    @pl.when(orb < n_orb - 1)
    def _():
        for copy in up:
            copy.start()

    @pl.when(orb > 0)
    def _():
        for copy in down:
            copy.start()

    @pl.when(orb == 0)
    def _():
        lo_v[...] = jnp.zeros_like(lo_v)
        lo_b[...] = jnp.zeros_like(lo_b)

    @pl.when(orb == n_orb - 1)
    def _():
        hi_v[...] = jnp.zeros_like(hi_v)
        hi_b[...] = jnp.zeros_like(hi_b)

    for j in inner:
        screen_block(j)

    def near_b(j, q):
        if j < 0:
            return lo_b[q]
        if j >= nbd:
            return hi_b[q]
        return kb[q, j * blk : (j + 1) * blk, :]

    def near_v(j):
        if j < 0:
            return lo_v[...]
        if j >= nbd:
            return hi_v[...]
        return kv[j * blk : (j + 1) * blk, :]

    def w_copy(p, c):
        cut = slice(c * piece, (c + 1) * piece)
        return pltpu.make_async_remote_copy(
            src_ref=own_w.at[p, :, cut, :],
            dst_ref=every_w.at[aux, :, cut, :],
            send_sem=w_send.at[p, c],
            recv_sem=w_recv.at[aux, c],
            device_id=(orb, p),
            device_id_type=MESH,
        )

    def one_block(j):
        def body(q, carry):
            terms = []
            for s in range(3):
                occ = ko[j * blk : (j + 1) * blk, s * blk : (s + 1) * blk]
                terms.append(
                    jnp.dot(occ, near_b(j + s - 1, q), preferred_element_type=jnp.float32)
                )
            for u in range(5):
                total = None
                for s in range(3):
                    t = u - s
                    if 0 <= t < 3:
                        piece = terms[s][:, t * blk : (t + 1) * blk]
                        total = piece if total is None else total + piece
                right[q, :, u * blk : (u + 1) * blk] = total.astype(jnp.bfloat16)
            return carry

        lax.fori_loop(0, aux_dev, body, 0)
        for s in range(3):
            rows_r = right[:, :, s * blk : s * blk + width].reshape(aux_dev * blk, width)
            value = lax.dot_general(
                rows_r,
                near_v(j + s - 1),
                (((1,), (1,)), ((), ())),
                preferred_element_type=jnp.float32,
            )
            value = (value * factor(bs_ref, j, s)).astype(jnp.bfloat16)
            value = value.reshape(aux_dev, blk, blk)
            for k in range(per_block):
                own_w[j * per_block + k, :, :, s * blk : (s + 1) * blk] = value[
                    :, k * share : (k + 1) * share
                ]
        for k in range(per_block):
            p = j * per_block + k

            @pl.when(aux != p)
            def _():
                w_copy(p, 0).start()

    for j in inner:
        one_block(j)

    @pl.when(orb > 0)
    def _():
        for copy in up:
            copy.wait_recv()

    @pl.when(orb < n_orb - 1)
    def _():
        for copy in down:
            copy.wait_recv()

    for j in edges:
        one_block(j)

    for c in range(1, pieces):
        for p in range(n_aux):

            @pl.when(aux != p)
            def _():
                w_copy(p, c).start()

    own_copy.wait()
    for copy in b_copies:
        copy.wait_recv()

    pair_rows = lax.broadcasted_iota(jnp.int32, (naux * TILE, aux_dev * TILE), 0)
    pair_cols = lax.broadcasted_iota(jnp.int32, (naux * TILE, aux_dev * TILE), 1)
    same = (pair_rows & (TILE - 1)) == (pair_cols & (TILE - 1))

    def products(ref, source, begin, end):
        total = None
        for t in range(begin // TILE, end // TILE):
            cut = slice(t * TILE, (t + 1) * TILE)
            left = every_b[:, :, cut, :].reshape(naux * TILE, width)
            other = ref[source, :, cut, :].reshape(aux_dev * TILE, width)
            term = lax.dot_general(
                left, other, (((1,), (1,)), ((), ())), preferred_element_type=jnp.float32
            )
            total = term if total is None else total + term
        return total

    def diagonal(total):
        total = jnp.where(same, total, 0.0).reshape(naux, TILE, aux_dev * TILE)
        return jnp.sum(total, axis=1)

    def placed(total, source):
        shape = (aux_dev * TILE, lanes)
        row = lax.broadcasted_iota(jnp.int32, shape, 0) // TILE
        col = lax.broadcasted_iota(jnp.int32, shape, 1)
        pick = jnp.where(row + source * aux_dev == col, 1.0, 0.0)
        value = jnp.dot(
            total, pick, precision=lax.Precision.HIGHEST, preferred_element_type=jnp.float32
        )
        return value.reshape(n_aux, aux_dev, lanes)

    part[...] = placed(diagonal(products(own_w, aux, 0, share)), aux)
    for c in range(pieces):
        cut = slice(c * piece, (c + 1) * piece)
        for k in range(1, n_aux):
            source = xor(aux, k, n_aux)
            pltpu.make_async_remote_copy(
                src_ref=own_w.at[source, :, cut, :],
                dst_ref=every_w.at[source, :, cut, :],
                send_sem=w_send.at[source, c],
                recv_sem=w_recv.at[source, c],
                device_id=(orb, source),
                device_id_type=MESH,
            ).wait_recv()
            total = products(every_w, source, c * piece, (c + 1) * piece)
            if c > 0:
                total = total + pair_acc[k]
            if c < pieces - 1:
                pair_acc[k] = total
            else:
                part[...] += placed(diagonal(total), source)

    p_copies = []
    for k in range(1, n_aux):
        peer = xor(aux, k, n_aux)
        copy = pltpu.make_async_remote_copy(
            src_ref=part.at[peer],
            dst_ref=part_aux.at[k],
            send_sem=p_send.at[k],
            recv_sem=p_recv.at[k],
            device_id=(orb, peer),
            device_id_type=MESH,
        )
        copy.start()
        p_copies.append(copy)
    mine = part[aux]
    for k in range(1, n_aux):
        p_copies[k - 1].wait_recv()
        mine = mine + part_aux[k]
    part_orb[orb] = mine
    q_copies = []
    for k in range(1, n_orb):
        peer = lax.rem(orb + k, n_orb)
        copy = pltpu.make_async_remote_copy(
            src_ref=part_orb.at[orb],
            dst_ref=part_orb.at[orb],
            send_sem=q_send.at[k],
            recv_sem=q_recv.at[k],
            device_id=(peer, aux),
            device_id_type=MESH,
        )
        copy.start()
        q_copies.append(copy)
    for k in range(1, n_orb):
        source = lax.rem(orb + n_orb - k, n_orb)
        pltpu.make_async_remote_copy(
            src_ref=part_orb.at[source],
            dst_ref=part_orb.at[source],
            send_sem=q_send.at[k],
            recv_sem=q_recv.at[k],
            device_id=(source, aux),
            device_id_type=MESH,
        ).wait_recv()
    result = part_orb[0]
    for k in range(1, n_orb):
        result = result + part_orb[k]
    out_ref[...] = result[:, :naux]

    for copy in b_copies + p_copies + q_copies:
        copy.wait_send()

    @pl.when(orb < n_orb - 1)
    def _():
        for copy in up:
            copy.wait_send()

    @pl.when(orb > 0)
    def _():
        for copy in down:
            copy.wait_send()

    for p in range(n_aux):

        @pl.when(aux != p)
        def _():
            for c in range(pieces):
                w_copy(p, c).wait_send()


def per_device(n_orb, n_aux, three_centre, b_screen, g_occ, occ_screen, g_vir, vir_screen):
    aux_dev, rows, width = three_centre.shape
    blk = width // 3
    share = rows // n_aux
    naux = n_aux * aux_dev
    pieces = min(4, share // TILE)
    lanes = -(-naux // ORDER_LANES) * ORDER_LANES
    bf16, f32 = jnp.bfloat16, jnp.float32
    anywhere = pl.BlockSpec(memory_space=pl.ANY)
    vmem = pl.BlockSpec(memory_space=pltpu.VMEM)
    smem = pl.BlockSpec(memory_space=pltpu.SMEM)
    dma = pltpu.SemaphoreType.DMA
    flops = 4 * aux_dev * rows * width * width
    return pl.pallas_call(
        functools.partial(kernel, n_orb, n_aux),
        out_shape=jax.ShapeDtypeStruct((aux_dev, naux), f32),
        in_specs=[anywhere, anywhere, anywhere, smem, smem, smem],
        out_specs=vmem,
        scratch_shapes=[
            pltpu.VMEM((aux_dev, rows, width), bf16),
            pltpu.VMEM((aux_dev, blk, width), bf16),
            pltpu.VMEM((aux_dev, blk, width), bf16),
            pltpu.VMEM((rows, width), bf16),
            pltpu.VMEM((rows, width), bf16),
            pltpu.VMEM((rows, width), bf16),
            pltpu.VMEM((rows, width), bf16),
            pltpu.VMEM((blk, width), bf16),
            pltpu.VMEM((blk, width), bf16),
            pltpu.VMEM((aux_dev, blk, 5 * blk), bf16),
            pltpu.VMEM((n_aux, aux_dev, share, width), bf16),
            pltpu.VMEM((n_aux, aux_dev, share, width), bf16),
            pltpu.VMEM((n_aux, aux_dev, share, width), bf16),
            pltpu.VMEM((n_aux, aux_dev, lanes), f32),
            pltpu.VMEM((n_aux, aux_dev, lanes), f32),
            pltpu.VMEM((n_orb, aux_dev, lanes), f32),
            dma((rows // blk,)),
            dma,
            dma((n_aux,)),
            dma((n_aux,)),
            dma((4,)),
            dma((4,)),
            dma((n_aux, pieces)),
            dma((n_aux, pieces)),
            dma((n_aux,)),
            dma((n_aux,)),
            dma((n_orb,)),
            dma((n_orb,)),
            dma((2,)),
            pltpu.VMEM((n_aux, naux * TILE, aux_dev * TILE), f32),
        ],
        compiler_params=pltpu.CompilerParams(
            collective_id=0, has_side_effects=True, vmem_limit_bytes=56 * 1024 * 1024
        ),
        cost_estimate=pl.CostEstimate(
            flops=flops, bytes_accessed=4 * aux_dev * rows * width, transcendentals=0
        ),
    )(three_centre, g_occ, g_vir, b_screen, occ_screen, vir_screen)


def solution(mesh):
    in_specs = (
        P("aux", "orb", None),
        P("orb", None),
        P("orb", None),
        P("orb", None),
        P("orb", None),
        P("orb", None),
    )
    out_specs = P("aux", None)
    body = functools.partial(per_device, mesh.shape["orb"], mesh.shape["aux"])
    return jax.shard_map(body, mesh=mesh, in_specs=in_specs, out_specs=out_specs, check_vma=False)
```
